32 devices in a mesh: row: 8 (over y, x, core), col: 4 (over z).
Axes of the slice: x: 2, y: 2, z: 4, core: 2. Of those that a mesh axis runs over, the one named last changes fastest.
Arguments:
- density: bfloat16 [8192, 8192], P('col', 'row'), may hold values from -0.09375 to 0.09375
- hamiltonian: bfloat16 [8192, 8192], P('row', 'col'), may hold values from -6 to 6
- pattern_p: int32 [64, 64], P('col', 'row'), may hold values 0 or 1
- pattern_h: int32 [64, 64], P('row', 'col'), may hold values 0 or 1
- pattern_s: int32 [8, 64], P('col', 'row'), may hold values 0 or 1
- owner: int32 [4, 8, 16, 1], P('col', 'row'), may hold values from 0 to 3; in each aligned block of 16 rows (0 to 15, 16 to 31, ..., all dimensions but the last counted through in order) at most 8 rows name the same one
- d_intersection: bfloat16 [8, 4, 3, 32, 128, 128], P('row', 'col'), may hold values from -6 to 6
- d_hamilton: bfloat16 [8, 4, 3, 32, 128, 128], P('row', 'col'), may hold values from -6 to 6
Outputs:
- weighted: bfloat16 [1024, 8192], P('col', 'row')
- forces: float32 [8, 4, 3, 32], P('row', 'col')
The draws below stay inside these ranges and needn't reach their ends.
Inputs may be any that keep to these rules, and one draw needn't show every extreme that they name: Among the 16 blocks of one device no owner is named more than 8 times.
All inputs are finite; a program needn't handle non-finite values. No bound on the sum of `pattern_p` or of `pattern_h` or of `pattern_s` on one device may be relied on, other than what follows from the above.
Results may differ from the reference program's by a relative error of at most 0.0049.
Values may be sent and summed in bfloat16 or wider, within the bound.
A program may use at most 128 MiB of HBM per device.

```python
import math
import jax
import jax.numpy as jnp
import numpy as np

BLOCK = 128
CBLK = 8
SBLK = 2
NB = 64
N = 8192
MB = 8
M = 1024
CAP = 8
SLOTS = 32
N_ROW = 8
N_COL = 4


def touch_ends(drawn, key, low, high):
    shape = drawn.shape
    index_at = [jax.random.randint(jax.random.fold_in(key, axis), (), 0, shape[axis]) for axis in range(len(shape))]
    drawn = drawn.at[tuple(index_at)].set(low)
    longest = shape.index(max(shape))
    index_at[longest] = (index_at[longest] + 1) % shape[longest]
    return drawn.at[tuple(index_at)].set(high)


def level_of(rng, extent, split, low, top_value):
    def one(dim, parts):
        steps = jax.random.uniform(jax.random.fold_in(jax.random.fold_in(rng, 6), dim), (parts,), jnp.float32, low / len(split), top_value / len(split))
        return jnp.repeat(jnp.exp(steps), extent[dim] // parts).reshape((-1,) + (1,) * (len(extent) - dim - 1))

    level = one(*split[0])
    for cut in split[1:]:
        level = level * one(*cut)
    return level


def routed_block(own_key, own, number, rows, amount, top, bound, skew):
    order = jax.random.permutation(own_key, amount)
    heavy_load, ordinary = shares(amount, rows * top, bound, skew, True), shares(amount, rows * top, bound, skew, False)
    places = jnp.arange(amount)

    def named(lengths, turn):
        used = int((lengths > 0).sum())
        fixed = max(1, used // 4)
        shifted = fixed + (places - fixed + turn * (used - fixed)) % max(1, amount - fixed)
        return jnp.zeros((amount,), jnp.int32).at[order[jnp.where(places < fixed, places, shifted)]].set(jnp.asarray(lengths, jnp.int32))

    lengths = jnp.where(number % 4 == 0, named(heavy_load, number // 4), named(ordinary, number - number // 4 - 1))
    mixed = jax.random.permutation(jax.random.fold_in(own, 3), amount)
    giver, taker = mixed[0:amount // 2 * 2:2], mixed[1:amount // 2 * 2:2]
    room = jnp.minimum(lengths[giver] - 1, bound - lengths[taker]) // 2
    room = jnp.where((giver == order[0]) | (taker == order[0]) | (lengths[taker] == 0), 0, jnp.maximum(room, 0))
    shifted = jax.random.randint(jax.random.fold_in(own, 4), (amount // 2,), 0, 1 << 20) % (room + 1)
    lengths = lengths.at[giver].add(-shifted).at[taker].add(shifted)
    labels = jnp.searchsorted(jnp.cumsum(lengths), jnp.arange(rows * top), side="right").astype(jnp.int32)
    listing = labels.reshape(top, rows).T
    listing = listing[jax.random.permutation(jax.random.fold_in(own, 1), rows)]
    turn = jax.random.randint(jax.random.fold_in(own, 2), (rows, 1), 0, top)
    return jnp.take_along_axis(listing, (jnp.arange(top)[None, :] + turn) % top, axis=1)


def shares(number_of, total, reach, slope, full):
    portions = [(1 << 20) // math.isqrt(standing ** slope) + 1 for standing in range(1, number_of + 1)]
    largest = reach if full else min(reach, max(-(-total // number_of), total * portions[0] // sum(portions)))
    least = 1 if total - largest >= number_of - 1 else 0
    counts, rest = [largest] + [least] * (number_of - 1), total - largest - least * (number_of - 1)
    while rest > 0:
        free = [i for i in range(1, number_of) if counts[i] < largest] or [i for i in range(1, number_of) if counts[i] < reach]
        whole, remaining = sum([portions[i] for i in free]), rest
        for i in free:
            extra = min(reach - counts[i], max(1, remaining * portions[i] // whole), rest)
            counts[i] = counts[i] + extra
            rest = rest - extra
    return np.array(counts)


def noise(own_key, shape, width, most, pieces=(), kind=jnp.bfloat16):
    drawn = width * jax.random.normal(own_key, shape, jnp.float32)
    if pieces:
        drawn = drawn * level_of(own_key, shape, pieces, -0.22, 0.18)
    return jnp.clip(drawn, -most, most).astype(kind)


def setup_inputs(seed: int = 0) -> dict:
    splits = jax.random.split(jax.random.key(seed), 9)
    density = noise(splits[0], (N, N), (N // 2) ** -0.5, 0.09375, ((0, 4), (1, 8)))
    hamiltonian = noise(splits[1], (N, N), 1.0, 6.0, ((0, 8), (1, 4)))
    pattern_p = touch_ends((jax.random.randint(splits[2], (NB, NB), 0, 2) < 1).astype(jnp.int32), jax.random.fold_in(splits[2], 1), 0, 1)
    pattern_h = touch_ends((jax.random.randint(splits[3], (NB, NB), 0, 2) < 1).astype(jnp.int32), jax.random.fold_in(splits[3], 1), 0, 1)
    pattern_s = touch_ends((jax.random.randint(splits[4], (MB, NB), 0, 2) < 1).astype(jnp.int32), jax.random.fold_in(splits[4], 1), 0, 1)
    owner_keys = jax.random.split(jax.random.fold_in(splits[5], 1), N_COL * N_ROW * (SBLK * CBLK) // (SBLK * CBLK))
    owner_turns = jax.random.permutation(jax.random.fold_in(splits[5], 3), N_COL * N_ROW * (SBLK * CBLK) // (SBLK * CBLK))
    owner = jax.vmap(lambda own, number: routed_block(jax.random.fold_in(splits[5], 2), own, number, SBLK * CBLK, N_COL, 1, CAP, 2))(owner_keys, owner_turns).reshape((N_COL, N_ROW, SBLK * CBLK, 1))
    d_intersection = noise(splits[6], (N_ROW, N_COL, 3, SLOTS, BLOCK, BLOCK), 1.0, 6.0, ((0, 8), (1, 4)))
    d_hamilton = noise(splits[7], (N_ROW, N_COL, 3, SLOTS, BLOCK, BLOCK), 1.0, 6.0, ((0, 8), (1, 4)))
    return dict(density=density, hamiltonian=hamiltonian, pattern_p=pattern_p, pattern_h=pattern_h, pattern_s=pattern_s, owner=owner, d_intersection=d_intersection, d_hamilton=d_hamilton)


def spread(matrix, pattern):
    rows, cols = matrix.shape
    rb, cb = pattern.shape
    tiles = matrix.reshape(rb, rows // rb, cb, cols // cb) * pattern[:, None, :, None].astype(matrix.dtype)
    return tiles.reshape(rows, cols)


def to_blocks(matrix):
    tiles = matrix.reshape(N_COL, SBLK, BLOCK, N_ROW, CBLK, BLOCK).transpose(3, 0, 1, 4, 2, 5)
    return tiles.reshape(N_ROW, N_COL, SBLK * CBLK, BLOCK * BLOCK).astype(jnp.float32)


def reference(density, hamiltonian, pattern_p, pattern_h, pattern_s, owner, d_intersection, d_hamilton):
    masked_p = spread(density, pattern_p)
    masked_h = spread(hamiltonian, pattern_h)
    slab = masked_p.reshape(N_COL, N // N_COL, N)[:, : SBLK * BLOCK, :].reshape(M, N)
    panel = jnp.dot(slab, masked_h, preferred_element_type=jnp.float32).astype(jnp.bfloat16)
    product = jnp.dot(panel, masked_p, preferred_element_type=jnp.float32)
    weighted = spread(product, pattern_s).astype(jnp.bfloat16)
    w_blocks = to_blocks(weighted)
    p_blocks = to_blocks(slab)
    target = owner.transpose(1, 0, 2, 3).reshape(N_ROW, N_COL, SBLK * CBLK)
    onehot = (target[..., None] == jnp.arange(N_COL, dtype=jnp.int32)).astype(jnp.int32)
    before = jnp.cumsum(onehot, axis=2) - onehot
    rank = jnp.sum(before * onehot, axis=3)
    slot_id = target * CAP + rank
    select = (slot_id[..., None] == jnp.arange(SLOTS, dtype=jnp.int32)).astype(jnp.float32)

    def route(blocks):
        sent = jnp.einsum("rcks,rckx->rcsx", select, blocks)
        sent = sent.reshape(N_ROW, N_COL, N_COL, CAP, BLOCK * BLOCK).transpose(0, 2, 1, 3, 4)
        return sent.reshape(N_ROW, N_COL, SLOTS, BLOCK * BLOCK)

    got_w = route(w_blocks)
    got_p = route(p_blocks)
    dov = d_intersection.astype(jnp.float32).reshape(N_ROW, N_COL, 3, SLOTS, BLOCK * BLOCK)
    dham = d_hamilton.astype(jnp.float32).reshape(N_ROW, N_COL, 3, SLOTS, BLOCK * BLOCK)
    first = jnp.einsum("rdzsx,rdsx->rdzs", dham, got_p)
    second = jnp.einsum("rdzsx,rdsx->rdzs", dov, got_w)
    forces = (first - second) / BLOCK
    return weighted, forces
```

```python
import functools

import jax
import jax.numpy as jnp
from jax import lax
from jax.experimental import pallas as pl
from jax.experimental.pallas import tpu as pltpu
from jax.sharding import PartitionSpec as P

BLOCK = 128
CBLK = 8
SBLK = 2
ROWS = SBLK * BLOCK
NBLK = SBLK * CBLK
BF = jnp.bfloat16
F32 = jnp.float32
MESH = pl.DeviceIdType.MESH


def spread(matrix, pattern):
    rows, cols = matrix.shape
    rb, cb = pattern.shape
    tiles = matrix.reshape(rb, rows // rb, cb, cols // cb) * pattern[:, None, :, None].astype(
        matrix.dtype
    )
    return tiles.reshape(rows, cols)


def rows_at(start, size):
    return pl.ds(pl.multiple_of(start, 16), size)


def main_kernel(nr, nc, cap, ps_ref, idx_ref, p_ref, h_ref, w_out, wr_out, pr_out,
                slab, acc, sbuf, rbuf, ybuf, wown, wrecv, blkp, blkw, op, ow, ip, iw,
                sl_s, sl_r, rs_s, rs_r, ag_s, ag_r, w_s, w_r, p_s, p_r, q_s, q_r):
    r = lax.axis_index("row")
    c = lax.axis_index("col")
    steps = nr.bit_length() - 1
    half = h_ref.shape[1] // 2
    bits = list(range(steps))
    orders = [bits, bits[:1] + bits[2:] + bits[1:2]]
    bit = [lax.rem(r // (1 << b), 2) for b in bits]
    mate = [r + (1 - 2 * bit[b]) * (1 << b) for b in bits]
    peer = [lax.rem(c + d, nc) for d in range(nc)]

    barrier = pltpu.get_barrier_semaphore()
    for b in bits:
        pl.semaphore_signal(barrier, inc=1, device_id=(mate[b], c), device_id_type=MESH)
    for d in range(1, nc):
        pl.semaphore_signal(barrier, inc=1, device_id=(r, peer[d]), device_id_type=MESH)
    pl.semaphore_wait(barrier, steps + nc - 1)

    def remote(src, dst, s, t, where):
        return pltpu.make_async_remote_copy(
            src_ref=src, dst_ref=dst, send_sem=s, recv_sem=t, device_id=where,
            device_id_type=MESH)

    order = sorted(range(nc), key=lambda d: (min(d, nc - d), d))
    slab_copy = {}
    for d in order[1:]:
        cp = remote(p_ref.at[pl.ds(0, ROWS)], slab.at[nc - d], sl_s.at[nc - d],
                    sl_r.at[nc - d], (r, peer[d]))
        cp.start()
        slab_copy[nc - d] = cp

    def route(blk, out, inn, s, t):
        copies = []
        for d in list(range(1, nc)) + [0]:
            def pick(q, carry, d=d):
                got = blk[idx_ref[peer[d] * cap + q]]
                if d == 0:
                    inn[c * cap + q] = got
                else:
                    out[d * cap + q] = got
                return carry
            lax.fori_loop(0, cap, pick, 0)
            if d:
                cp = remote(out.at[pl.ds(d * cap, cap)], inn.at[pl.ds(c * cap, cap)],
                            s.at[d], t.at[d], (r, peer[d]))
                cp.start()
                copies.append(cp)
        return copies

    rel = []
    for s in range(2):
        at = [0]
        for k in range(1, steps):
            at.append(at[-1] + bit[orders[s][k]] * (ROWS >> (k + 1)))
        rel.append([None] + at)
    base = bit[0] * (ROWS // 2)
    rs = {}
    ag = {}
    wc = {}

    def region(k):
        return pl.ds(ROWS - (ROWS >> k), ROWS >> (k + 1))

    def first(j):
        if j:
            slab_copy[j].wait()
        for send in (True, False):
            start = ROWS // 2 - base if send else base
            for s in range(2):
                def tile(t, carry, s=s, send=send, start=start):
                    cols = pl.ds(pl.multiple_of(t * 256, 256), 256)
                    hcol = pl.ds(pl.multiple_of(s * half + t * 256, 256), 256)
                    rows = rows_at(start, ROWS // 2)
                    a = slab[j, rows, :] if j else p_ref[rows, :]
                    v = jnp.dot(a, h_ref[:, hcol], preferred_element_type=F32)
                    if send:
                        sbuf[j, s, pl.ds(0, ROWS // 2), cols] = v.astype(BF)
                    else:
                        acc[j, s, :, cols] = v
                    return carry
                lax.fori_loop(0, half // 256, tile, 0)
                if send:
                    start_rs(j, s, 0)

    def start_rs(j, s, k):
        cp = remote(sbuf.at[j, s, region(k)], rbuf.at[j, s, region(k)], rs_s.at[j, s, k],
                    rs_r.at[j, s, k], (mate[orders[s][k]], c))
        cp.start()
        rs[j, s, k] = cp

    def reduce(j, k):
        for s in range(2):
            rs[j, s, k - 1].wait()
            size = ROWS >> k
            came = ROWS - (ROWS >> (k - 1))
            at = rel[s][k]
            if k == steps:
                def last(i, carry, s=s, at=at):
                    x = acc[j, s, rows_at(at + i * 16, 16), :]
                    y = rbuf[j, s, pl.ds(pl.multiple_of(came + i * 16, 16), 16), :].astype(F32)
                    ybuf[j, s, rows_at(base + at + i * 16, 16), :] = (x + y).astype(BF)
                    return carry
                lax.fori_loop(0, size // 16, last, 0)
                start_ag(j, s, k - 1)
            else:
                h = size // 2
                away = (1 - bit[orders[s][k]]) * h
                keep = bit[orders[s][k]] * h
                for off, send in ((away, True), (keep, False)):
                    def add(i, carry, s=s, at=at, off=off, send=send):
                        rows = rows_at(at + off + i * 16, 16)
                        y = rbuf[j, s, rows_at(came + off + i * 16, 16), :].astype(F32)
                        v = acc[j, s, rows, :] + y
                        if send:
                            sbuf[j, s, rows_at(ROWS - (ROWS >> k) + i * 16, 16), :] = v.astype(BF)
                        else:
                            acc[j, s, rows, :] = v
                        return carry
                    lax.fori_loop(0, h // 16, add, 0)
                    if send:
                        start_rs(j, s, k)

    def start_ag(j, s, k):
        seg = rows_at(base + rel[s][k + 1], ROWS >> (k + 1))
        cp = remote(ybuf.at[j, s, seg], ybuf.at[j, s, seg], ag_s.at[j, s, k], ag_r.at[j, s, k],
                    (mate[orders[s][k]], c))
        cp.start()
        ag[j, s, k] = cp

    def gather(j, k):
        for s in range(2):
            ag[j, s, k].wait()
            start_ag(j, s, k - 1)

    def second(j):
        for s in range(2):
            ag[j, s, 0].wait()

        def tile(t, carry):
            cols = pl.ds(pl.multiple_of(t * 256, 256), 256)
            v = jnp.dot(ybuf[j, 0], p_ref[pl.ds(0, half), cols], preferred_element_type=F32)
            v = v + jnp.dot(ybuf[j, 1], p_ref[pl.ds(half, half), cols],
                            preferred_element_type=F32)
            if j:
                sbuf[j, 0, :, cols] = v.astype(BF)
            else:
                wown[:, cols] = v
            return carry
        lax.fori_loop(0, CBLK * BLOCK // 256, tile, 0)
        if j:
            cp = remote(sbuf.at[j, 0], wrecv.at[j], w_s.at[j], w_r.at[j], (r, peer[j]))
            cp.start()
            wc[j] = cp

    stages = [first]
    stages += [functools.partial(lambda j, k: reduce(j, k), k=k) for k in range(1, steps + 1)]
    stages += [functools.partial(lambda j, k: gather(j, k), k=k) for k in range(steps - 1, 0, -1)]
    stages += [second]
    pcopies = []
    for t in range(nc + len(stages) - 1):
        for i in range(nc):
            if 0 <= t - i < len(stages):
                stages[t - i](order[i])
        if t == 0:
            for u in range(SBLK):
                for v in range(CBLK):
                    blkp[u * CBLK + v] = p_ref[pl.ds(u * BLOCK, BLOCK), pl.ds(v * BLOCK, BLOCK)]
            blkp[NBLK] = jnp.zeros((BLOCK, BLOCK), BF)
            blkw[NBLK] = jnp.zeros((BLOCK, BLOCK), BF)
        if t == nc - 1:
            pcopies = route(blkp, op, ip, p_s, p_r)

    for d in order[1:]:
        wc[d].wait()
    for u in range(SBLK):
        for v in range(CBLK):
            rows, cols = pl.ds(u * BLOCK, BLOCK), pl.ds(v * BLOCK, BLOCK)
            x = wown[rows, cols]
            for d in range(1, nc):
                x = x + wrecv[d, rows, cols].astype(F32)
            blkw[u * CBLK + v] = (x * ps_ref[u, v].astype(F32)).astype(BF)
    wcopies = route(blkw, ow, iw, q_s, q_r)
    for u in range(SBLK):
        for v in range(CBLK):
            w_out[pl.ds(u * BLOCK, BLOCK), pl.ds(v * BLOCK, BLOCK)] = blkw[u * CBLK + v]
    for cp in pcopies:
        cp.wait()

    def copy_p(i, carry):
        pr_out[i] = ip[i]
        return carry
    lax.fori_loop(0, nc * cap, copy_p, 0)
    for cp in wcopies:
        cp.wait()

    def copy_w(i, carry):
        wr_out[i] = iw[i]
        return carry
    lax.fori_loop(0, nc * cap, copy_w, 0)


def force_kernel(dh_ref, ds_ref, pr_ref, wr_ref, out_ref):
    for q in range(dh_ref.shape[1]):
        p = pr_ref[q].astype(F32)
        w = wr_ref[q].astype(F32)
        for z in range(3):
            t = dh_ref[z, q].astype(F32) * p - ds_ref[z, q].astype(F32) * w
            out_ref[z, q:q + 1, :] = jnp.sum(t, axis=0, keepdims=True)


def local(nr, nc, density, hamiltonian, pattern_p, pattern_h, pattern_s, owner, d_intersection,
          d_hamilton):
    masked_p = spread(density, pattern_p)
    masked_h = spread(hamiltonian, pattern_h)
    slots = d_intersection.shape[3]
    cap = slots // nc
    steps = nr.bit_length() - 1
    target = owner.reshape(NBLK)
    same = target[:, None] == target[None, :]
    number = jnp.arange(NBLK, dtype=jnp.int32)
    rank = jnp.sum(jnp.where(same & (number[None, :] < number[:, None]), 1, 0), axis=1)
    hit = jnp.arange(slots, dtype=jnp.int32)[:, None] == (target * cap + rank)[None, :]
    index = NBLK + jnp.sum(jnp.where(hit, number[None, :] - NBLK, 0), axis=1)
    half = hamiltonian.shape[1] // 2
    width = CBLK * BLOCK
    sem = pltpu.SemaphoreType.DMA
    smem = pl.BlockSpec(memory_space=pltpu.SMEM)
    vmem = pl.BlockSpec(memory_space=pltpu.VMEM)
    block = (BLOCK, BLOCK)
    weighted, wr, pr = pl.pallas_call(
        functools.partial(main_kernel, nr, nc, cap),
        out_shape=(jax.ShapeDtypeStruct((ROWS, width), BF),
                   jax.ShapeDtypeStruct((slots,) + block, BF),
                   jax.ShapeDtypeStruct((slots,) + block, BF)),
        in_specs=[smem, smem, vmem, vmem],
        out_specs=(vmem, vmem, vmem),
        scratch_shapes=[
            pltpu.VMEM((nc, ROWS, width), BF),
            pltpu.VMEM((nc, 2, ROWS // 2, half), F32),
            pltpu.VMEM((nc, 2, ROWS, half), BF),
            pltpu.VMEM((nc, 2, ROWS, half), BF),
            pltpu.VMEM((nc, 2, ROWS, half), BF),
            pltpu.VMEM((ROWS, width), F32),
            pltpu.VMEM((nc, ROWS, width), BF),
            pltpu.VMEM((NBLK + 1,) + block, BF),
            pltpu.VMEM((NBLK + 1,) + block, BF),
            pltpu.VMEM((slots,) + block, BF),
            pltpu.VMEM((slots,) + block, BF),
            pltpu.VMEM((slots,) + block, BF),
            pltpu.VMEM((slots,) + block, BF),
            sem((nc,)), sem((nc,)),
            sem((nc, 2, steps)), sem((nc, 2, steps)),
            sem((nc, 2, steps)), sem((nc, 2, steps)),
            sem((nc,)), sem((nc,)), sem((nc,)), sem((nc,)), sem((nc,)), sem((nc,)),
        ],
        compiler_params=pltpu.CompilerParams(
            collective_id=0, has_side_effects=True, vmem_limit_bytes=63 * 2**20),
        name="density_product",
    )(pattern_s, index, masked_p, masked_h)
    group = 8
    sums = pl.pallas_call(
        force_kernel,
        grid=(slots // group,),
        out_shape=jax.ShapeDtypeStruct((3, slots, BLOCK), F32),
        in_specs=[pl.BlockSpec((3, group) + block, lambda i: (0, i, 0, 0)),
                  pl.BlockSpec((3, group) + block, lambda i: (0, i, 0, 0)),
                  pl.BlockSpec((group,) + block, lambda i: (i, 0, 0)),
                  pl.BlockSpec((group,) + block, lambda i: (i, 0, 0))],
        out_specs=pl.BlockSpec((3, group, BLOCK), lambda i: (0, i, 0)),
        name="pair_forces",
    )(d_hamilton.reshape((3, slots) + block), d_intersection.reshape((3, slots) + block), pr, wr)
    forces = jnp.sum(sums, axis=-1) / BLOCK
    return (weighted, forces.reshape(1, 1, 3, slots))


def solution(mesh):
    nr, nc = mesh.shape["row"], mesh.shape["col"]
    in_specs = (
        P("col", "row"),
        P("row", "col"),
        P("col", "row"),
        P("row", "col"),
        P("col", "row"),
        P("col", "row", None, None),
        P("row", "col", None, None, None, None),
        P("row", "col", None, None, None, None),
    )
    out_specs = (P("col", "row"), P("row", "col", None, None))
    return jax.shard_map(functools.partial(local, nr, nc), mesh=mesh, in_specs=in_specs,
                         out_specs=out_specs, check_vma=False)
```

```python
import functools

import jax
import jax.numpy as jnp
from jax import lax
from jax.experimental import pallas as pl
from jax.experimental.pallas import tpu as pltpu
from jax.sharding import PartitionSpec as P

BLOCK = 128
CBLK = 8
SBLK = 2
ROWS = SBLK * BLOCK
NBLK = SBLK * CBLK
BF = jnp.bfloat16
F32 = jnp.float32
MESH = pl.DeviceIdType.MESH


def rows_at(start, size):
    return pl.ds(pl.multiple_of(start, 16), size)


def main_kernel(nr, nc, cap, ps_ref, idx_ref, pp_ref, ph_ref, p_hbm, h_hbm, w_out, wr_out,
                pr_out, p_ref, h_ref, ld, slab, acc, sbuf, rbuf, ybuf, wown, wrecv, blkp, blkw, op, ow, ip, iw,
                sl_s, sl_r, rs_s, rs_r, ag_s, ag_r, w_s, w_r, p_s, p_r, q_s, q_r):
    r = lax.axis_index("row")
    c = lax.axis_index("col")
    steps = nr.bit_length() - 1
    half = h_ref.shape[1] // 2
    bits = list(range(steps))
    orders = [bits, bits[:1] + bits[2:] + bits[1:2]]
    bit = [lax.rem(r // (1 << b), 2) for b in bits]
    mate = [r + (1 - 2 * bit[b]) * (1 << b) for b in bits]
    peer = [lax.rem(c + d, nc) for d in range(nc)]

    depth = p_ref.shape[0]
    loads = [
        pltpu.make_async_copy(p_hbm.at[pl.ds(0, ROWS)], p_ref.at[pl.ds(0, ROWS)], ld.at[0]),
        pltpu.make_async_copy(h_hbm, h_ref, ld.at[1]),
        pltpu.make_async_copy(p_hbm.at[pl.ds(ROWS, depth - ROWS)],
                              p_ref.at[pl.ds(ROWS, depth - ROWS)], ld.at[2]),
    ]
    for load in loads:
        load.start()

    def mask(ref, pattern, low, high):
        def line(a, carry):
            rows = pl.ds(pl.multiple_of(a * BLOCK, BLOCK), BLOCK)
            for b in range(ref.shape[1] // BLOCK):
                cols = pl.ds(b * BLOCK, BLOCK)
                ref[rows, cols] = (ref[rows, cols].astype(F32)
                                   * pattern[a, b].astype(F32)).astype(BF)
            return carry
        lax.fori_loop(low, high, line, 0)

    left = (nc - 1 - 2 * c + nc) // nc
    near = left * c + (1 - left) * (nc - 1 - c)
    jd = [0]
    for i in range(1, nc):
        far = (i - 2 * near - 1 + nc) // nc
        ahead = (i + 1) // 2 if i % 2 else nc - i // 2
        d = i - near
        jd.append(far * (left * d + (1 - left) * (nc - d)) + (1 - far) * ahead)

    loads[0].wait()
    mask(p_ref, pp_ref, 0, SBLK)
    barrier = pltpu.get_barrier_semaphore()
    for b in bits:
        pl.semaphore_signal(barrier, inc=1, device_id=(mate[b], c), device_id_type=MESH)
    for d in range(1, nc):
        pl.semaphore_signal(barrier, inc=1, device_id=(r, peer[d]), device_id_type=MESH)
    pl.semaphore_wait(barrier, steps + nc - 1)

    def remote(src, dst, s, t, where):
        return pltpu.make_async_remote_copy(
            src_ref=src, dst_ref=dst, send_sem=s, recv_sem=t, device_id=where,
            device_id_type=MESH)

    own = p_ref.at[pl.ds(0, ROWS)]
    to_right = remote(own, slab.at[nc - 1], sl_s.at[0], sl_r.at[nc - 1], (r, c + 1))
    to_left = remote(own, slab.at[1], sl_s.at[nc], sl_r.at[1], (r, c - 1))
    sent = [(c + 1 < nc, to_right), (c > 0, to_left)]
    for there, cp in sent:
        pl.when(there)(cp.start)

    def arrive(i):
        j = jd[i]
        step = 2 * ((c + j) // nc) - 1
        cp = remote(slab.at[j], slab.at[j - step], sl_s.at[i], sl_r.at[j - step], (r, c + step))
        come = remote(own, slab.at[j], sl_s.at[i], sl_r.at[j], (r, peer[1]))
        come.wait_recv()
        there = (c + step >= 0) & (c + step < nc)
        pl.when(there)(cp.start)
        sent.append((there, cp))

    def route(blk, out, inn, s, t):
        copies = []
        for d in list(range(1, nc)) + [0]:
            def pick(q, carry, d=d):
                got = blk[idx_ref[peer[d] * cap + q]]
                if d == 0:
                    inn[c * cap + q] = got
                else:
                    out[d * cap + q] = got
                return carry
            lax.fori_loop(0, cap, pick, 0)
            if d:
                cp = remote(out.at[pl.ds(d * cap, cap)], inn.at[pl.ds(c * cap, cap)],
                            s.at[d], t.at[d], (r, peer[d]))
                cp.start()
                copies.append(cp)
        return copies

    rel = []
    for s in range(2):
        at = [0]
        for k in range(1, steps):
            at.append(at[-1] + bit[orders[s][k]] * (ROWS >> (k + 1)))
        rel.append([None] + at)
    base = bit[0] * (ROWS // 2)
    rs = {}
    ag = {}
    wc = {}

    def region(k):
        return pl.ds(ROWS - (ROWS >> k), ROWS >> (k + 1))

    def first(j):
        if j:
            arrive(j)
        for send in (True, False):
            start = ROWS // 2 - base if send else base
            for s in range(2):
                def tile(t, carry, s=s, send=send, start=start):
                    cols = pl.ds(pl.multiple_of(t * 256, 256), 256)
                    hcol = pl.ds(pl.multiple_of(s * half + t * 256, 256), 256)
                    rows = rows_at(start, ROWS // 2)
                    a = slab[jd[j], rows, :] if j else p_ref[rows, :]
                    v = jnp.dot(a, h_ref[:, hcol], preferred_element_type=F32)
                    if send:
                        sbuf[j, s, pl.ds(0, ROWS // 2), cols] = v.astype(BF)
                    else:
                        acc[j, s, :, cols] = v
                    return carry
                lax.fori_loop(0, half // 256, tile, 0)
                if send:
                    start_rs(j, s, 0)

    def start_rs(j, s, k):
        cp = remote(sbuf.at[j, s, region(k)], rbuf.at[j, s, region(k)], rs_s.at[j, s, k],
                    rs_r.at[j, s, k], (mate[orders[s][k]], c))
        cp.start()
        rs[j, s, k] = cp

    def reduce(j, k):
        for s in range(2):
            rs[j, s, k - 1].wait()
            size = ROWS >> k
            came = ROWS - (ROWS >> (k - 1))
            at = rel[s][k]
            if k == steps:
                def last(i, carry, s=s, at=at):
                    x = acc[j, s, rows_at(at + i * 16, 16), :]
                    y = rbuf[j, s, pl.ds(pl.multiple_of(came + i * 16, 16), 16), :].astype(F32)
                    ybuf[j, s, rows_at(base + at + i * 16, 16), :] = (x + y).astype(BF)
                    return carry
                lax.fori_loop(0, size // 16, last, 0)
                start_ag(j, s, k - 1)
            else:
                h = size // 2
                away = (1 - bit[orders[s][k]]) * h
                keep = bit[orders[s][k]] * h
                for off, send in ((away, True), (keep, False)):
                    def add(i, carry, s=s, at=at, off=off, send=send):
                        rows = rows_at(at + off + i * 16, 16)
                        y = rbuf[j, s, rows_at(came + off + i * 16, 16), :].astype(F32)
                        v = acc[j, s, rows, :] + y
                        if send:
                            sbuf[j, s, rows_at(ROWS - (ROWS >> k) + i * 16, 16), :] = v.astype(BF)
                        else:
                            acc[j, s, rows, :] = v
                        return carry
                    lax.fori_loop(0, h // 16, add, 0)
                    if send:
                        start_rs(j, s, k)

    def start_ag(j, s, k):
        seg = rows_at(base + rel[s][k + 1], ROWS >> (k + 1))
        cp = remote(ybuf.at[j, s, seg], ybuf.at[j, s, seg], ag_s.at[j, s, k], ag_r.at[j, s, k],
                    (mate[orders[s][k]], c))
        cp.start()
        ag[j, s, k] = cp

    def gather(j, k):
        for s in range(2):
            ag[j, s, k].wait()
            start_ag(j, s, k - 1)

    def second(j):
        for s in range(2):
            ag[j, s, 0].wait()

        def tile(t, carry):
            cols = pl.ds(pl.multiple_of(t * 256, 256), 256)
            v = jnp.dot(ybuf[j, 0], p_ref[pl.ds(0, half), cols], preferred_element_type=F32)
            v = v + jnp.dot(ybuf[j, 1], p_ref[pl.ds(half, half), cols],
                            preferred_element_type=F32)
            if j:
                sbuf[j, 0, :, cols] = v.astype(BF)
            else:
                wown[:, cols] = v
            return carry
        lax.fori_loop(0, CBLK * BLOCK // 256, tile, 0)
        if j:
            cp = remote(sbuf.at[j, 0], wrecv.at[jd[j]], w_s.at[j], w_r.at[jd[j]],
                        (r, lax.rem(c + jd[j], nc)))
            cp.start()
            wc[j] = cp

    stages = [first]
    stages += [functools.partial(lambda j, k: reduce(j, k), k=k) for k in range(1, steps + 1)]
    stages += [functools.partial(lambda j, k: gather(j, k), k=k) for k in range(steps - 1, 0, -1)]
    stages += [second]
    pcopies = []
    loads[1].wait()
    mask(h_ref, ph_ref, 0, h_ref.shape[0] // BLOCK)
    for t in range(nc + len(stages) - 1):
        for i in range(nc):
            if 0 <= t - i < len(stages):
                stages[t - i](i)
        if t == 0:
            loads[2].wait()
            mask(p_ref, pp_ref, SBLK, depth // BLOCK)
            for u in range(SBLK):
                for v in range(CBLK):
                    blkp[u * CBLK + v] = p_ref[pl.ds(u * BLOCK, BLOCK), pl.ds(v * BLOCK, BLOCK)]
            blkp[NBLK] = jnp.zeros((BLOCK, BLOCK), BF)
            blkw[NBLK] = jnp.zeros((BLOCK, BLOCK), BF)
        if t == nc - 1:
            pcopies = route(blkp, op, ip, p_s, p_r)

    for there, cp in sent:
        pl.when(there)(cp.wait_send)
    for d in range(1, nc):
        wc[d].wait()
    for u in range(SBLK):
        for v in range(CBLK):
            rows, cols = pl.ds(u * BLOCK, BLOCK), pl.ds(v * BLOCK, BLOCK)
            x = wown[rows, cols]
            for d in range(1, nc):
                x = x + wrecv[d, rows, cols].astype(F32)
            blkw[u * CBLK + v] = (x * ps_ref[u, v].astype(F32)).astype(BF)
    wcopies = route(blkw, ow, iw, q_s, q_r)
    for u in range(SBLK):
        for v in range(CBLK):
            w_out[pl.ds(u * BLOCK, BLOCK), pl.ds(v * BLOCK, BLOCK)] = blkw[u * CBLK + v]
    for cp in pcopies:
        cp.wait()

    def copy_p(i, carry):
        pr_out[i] = ip[i]
        return carry
    lax.fori_loop(0, nc * cap, copy_p, 0)
    for cp in wcopies:
        cp.wait()

    def copy_w(i, carry):
        wr_out[i] = iw[i]
        return carry
    lax.fori_loop(0, nc * cap, copy_w, 0)


def force_kernel(dh_ref, ds_ref, pr_ref, wr_ref, out_ref):
    for q in range(dh_ref.shape[1]):
        p = pr_ref[q].astype(F32)
        w = wr_ref[q].astype(F32)
        for z in range(3):
            t = dh_ref[z, q].astype(F32) * p - ds_ref[z, q].astype(F32) * w
            out_ref[z, q:q + 1, :] = jnp.sum(t, axis=0, keepdims=True)


def local(nr, nc, density, hamiltonian, pattern_p, pattern_h, pattern_s, owner, d_intersection,
          d_hamilton):
    slots = d_intersection.shape[3]
    cap = slots // nc
    steps = nr.bit_length() - 1
    target = owner.reshape(NBLK)
    same = target[:, None] == target[None, :]
    number = jnp.arange(NBLK, dtype=jnp.int32)
    rank = jnp.sum(jnp.where(same & (number[None, :] < number[:, None]), 1, 0), axis=1)
    hit = jnp.arange(slots, dtype=jnp.int32)[:, None] == (target * cap + rank)[None, :]
    index = NBLK + jnp.sum(jnp.where(hit, number[None, :] - NBLK, 0), axis=1)
    half = hamiltonian.shape[1] // 2
    width = CBLK * BLOCK
    sem = pltpu.SemaphoreType.DMA
    smem = pl.BlockSpec(memory_space=pltpu.SMEM)
    vmem = pl.BlockSpec(memory_space=pltpu.VMEM)
    block = (BLOCK, BLOCK)
    weighted, wr, pr = pl.pallas_call(
        functools.partial(main_kernel, nr, nc, cap),
        out_shape=(jax.ShapeDtypeStruct((ROWS, width), BF),
                   jax.ShapeDtypeStruct((slots,) + block, BF),
                   jax.ShapeDtypeStruct((slots,) + block, BF)),
        in_specs=[smem] * 4 + [pl.BlockSpec(memory_space=pl.ANY)] * 2,
        out_specs=(vmem, vmem, vmem),
        scratch_shapes=[
            pltpu.VMEM(density.shape, BF), pltpu.VMEM(hamiltonian.shape, BF), sem((3,)),
            pltpu.VMEM((nc, ROWS, width), BF),
            pltpu.VMEM((nc, 2, ROWS // 2, half), F32),
            pltpu.VMEM((nc, 2, ROWS, half), BF),
            pltpu.VMEM((nc, 2, ROWS, half), BF),
            pltpu.VMEM((nc, 2, ROWS, half), BF),
            pltpu.VMEM((ROWS, width), F32),
            pltpu.VMEM((nc, ROWS, width), BF),
            pltpu.VMEM((NBLK + 1,) + block, BF),
            pltpu.VMEM((NBLK + 1,) + block, BF),
            pltpu.VMEM((slots,) + block, BF),
            pltpu.VMEM((slots,) + block, BF),
            pltpu.VMEM((slots,) + block, BF),
            pltpu.VMEM((slots,) + block, BF),
            sem((nc + 1,)), sem((nc,)),
            sem((nc, 2, steps)), sem((nc, 2, steps)),
            sem((nc, 2, steps)), sem((nc, 2, steps)),
            sem((nc,)), sem((nc,)), sem((nc,)), sem((nc,)), sem((nc,)), sem((nc,)),
        ],
        compiler_params=pltpu.CompilerParams(
            collective_id=0, has_side_effects=True, vmem_limit_bytes=63 * 2**20),
        name="density_product",
    )(pattern_s, index, pattern_p, pattern_h, density, hamiltonian)
    group = 8
    sums = pl.pallas_call(
        force_kernel,
        grid=(slots // group,),
        out_shape=jax.ShapeDtypeStruct((3, slots, BLOCK), F32),
        in_specs=[pl.BlockSpec((3, group) + block, lambda i: (0, i, 0, 0)),
                  pl.BlockSpec((3, group) + block, lambda i: (0, i, 0, 0)),
                  pl.BlockSpec((group,) + block, lambda i: (i, 0, 0)),
                  pl.BlockSpec((group,) + block, lambda i: (i, 0, 0))],
        out_specs=pl.BlockSpec((3, group, BLOCK), lambda i: (0, i, 0)),
        name="pair_forces",
    )(d_hamilton.reshape((3, slots) + block), d_intersection.reshape((3, slots) + block), pr, wr)
    forces = jnp.sum(sums, axis=-1) / BLOCK
    return (weighted, forces.reshape(1, 1, 3, slots))


def solution(mesh):
    nr, nc = mesh.shape["row"], mesh.shape["col"]
    in_specs = (
        P("col", "row"),
        P("row", "col"),
        P("col", "row"),
        P("row", "col"),
        P("col", "row"),
        P("col", "row", None, None),
        P("row", "col", None, None, None, None),
        P("row", "col", None, None, None, None),
    )
    out_specs = (P("col", "row"), P("row", "col", None, None))
    return jax.shard_map(functools.partial(local, nr, nc), mesh=mesh, in_specs=in_specs,
                         out_specs=out_specs, check_vma=False)
```
